32 devices in a mesh: node: 8 (over z, x), shard: 4 (over y, core).
Axes of the slice: x: 2, y: 2, z: 4, core: 2. Of those that a mesh axis runs over, the one named last changes fastest.
Arguments:
- hidden: bfloat16 [8, 512, 7168], P('node', 'shard'), may hold values from -6 to 6
- cotangent: bfloat16 [8, 512, 2048], P('node', 'shard'), may hold values from -0.25 to 0.25
- weights: bfloat16 [8, 7168, 2048], P('node', 'shard'), may hold values from -0.59765625 to 0.59765625
- momentum: bfloat16 [8, 7168, 2048], P('node', 'shard'), may hold values from -6 to 6
Outputs:
- new_weights: bfloat16 [8, 7168, 2048], P('node', 'shard')
- new_momentum: bfloat16 [8, 7168, 2048], P('node', 'shard')
The draws below stay inside these ranges and needn't reach their ends.
All inputs are finite; a program needn't handle non-finite values.
Results may differ from the reference program's by a relative error of at most 0.0085.
Values may be sent and summed in bfloat16 or wider, within the bound.
A program may use at most 64 MiB of HBM per device.

```python
import jax
import jax.numpy as jnp
from jax import lax

FFW = 7168
DW = 2048
TOKENS = 512
NODES = 8
N_NODE = 8


def steps_of(rng, extent, split, least, top_value):
    gain, own = 1.0, jax.random.fold_in(rng, 6)
    for position, parts in split:
        heights = jnp.exp(jax.random.uniform(jax.random.fold_in(own, position), (parts,), jnp.float32, least / len(split), top_value / len(split)))
        gain = gain * jnp.repeat(heights, extent[position] // parts).reshape([-1 if axis == position else 1 for axis in range(len(extent))])
    return gain


def normal_values(stream_key, extent, deviation, most, pieces=(), kind=jnp.bfloat16):
    gain = steps_of(stream_key, extent, pieces, -0.22, 0.18) if pieces else 1.0
    drawn = jax.random.normal(stream_key, extent, jnp.float32) * deviation * gain
    return jnp.minimum(jnp.maximum(drawn, -most), most).astype(kind)


def setup_inputs(seed: int = 0) -> dict:
    streams_of = jax.random.split(jax.random.key(seed), 5)
    return {
        "hidden": normal_values(streams_of[0], (NODES, TOKENS, FFW), 1.0, 6.0, ((0, 8), (1, 4))),
        "cotangent": normal_values(streams_of[1], (NODES, TOKENS, DW), TOKENS ** -0.5, 0.25, ((0, 8), (1, 4))),
        "weights": normal_values(streams_of[2], (NODES, FFW, DW), 0.1, 0.59765625, ((0, 8), (1, 4))),
        "momentum": normal_values(streams_of[3], (NODES, FFW, DW), 1.0, 6.0, ((0, 8), (1, 4))),
    }


step_size = 0.1
friction = 0.9


def reference(hidden, cotangent, weights, momentum):
    node_ids = jnp.arange(N_NODE, dtype=jnp.int32)

    def update(node):
        gradient = lax.dot_general(hidden[node], cotangent[node], (((0,), (0,)), ((), ())), preferred_element_type=jnp.float32)
        new_moment = (friction * momentum[node].astype(jnp.float32) + gradient).astype(jnp.bfloat16)
        kept = lax.optimization_barrier(new_moment)
        half_step = (weights[node].astype(jnp.float32) - step_size * kept.astype(jnp.float32)).astype(jnp.bfloat16)
        return new_moment, half_step

    moment_all, half_all = lax.map(update, node_ids)
    half_all = lax.optimization_barrier(half_all)
    row_count = N_NODE // 4

    def trimmed(node):
        row_pos = node // 4
        col_pos = node % 4
        others = [node,
                  row_pos * 4 + (col_pos + 1) % 4,
                  row_pos * 4 + (col_pos + 3) % 4,
                  ((row_pos + 1) % row_count) * 4 + col_pos,
                  ((row_pos + row_count - 1) % row_count) * 4 + col_pos]
        candidates = [half_all[other].astype(jnp.float32) for other in others]
        running = candidates[0]
        largest = candidates[0]
        smallest = candidates[0]
        for value in candidates[1:]:
            running = running + value
            largest = jnp.maximum(largest, value)
            smallest = jnp.minimum(smallest, value)
        return ((running - largest - smallest) / 3.0).astype(jnp.bfloat16)

    new_weights = lax.map(trimmed, node_ids)
    return new_weights, moment_all
```

```python
import functools

import jax
import jax.numpy as jnp
from jax import lax
from jax.experimental import pallas as pl
from jax.experimental.pallas import tpu as pltpu
from jax.sharding import PartitionSpec as P

step_size = 0.1
friction = 0.9
RELAY_LAG = 1
FINAL_LAG = 6


def flip(index, bit):
    return index + bit - 2 * bit * lax.rem(lax.div(index, bit), 2)


def largest_block(extent, unit, most):
    block = unit
    for size in range(unit, most + 1, unit):
        if extent % size == 0:
            block = size
    return block


def kernel(
    nodes, shards, rows, cols,
    hidden, cotangent, weights, momentum, new_weights, new_moment,
    acts, grads, w_tiles, m_tiles, h_tiles, west, east, north, south, product,
    acts_own, acts_send, acts_recv, grads_own, grads_send, grads_recv,
    w_sem, m_sem, west_send, west_recv, east_send, east_recv,
    north_send, north_recv, south_send, south_recv,
):
    node = lax.axis_index("node")
    shard = lax.axis_index("shard")
    row_parts, tokens, _ = acts.shape
    col_parts = grads.shape[0]
    own_tokens = tokens // shards
    tiles = row_parts * col_parts
    own_rows = rows * row_parts
    four_rows = nodes == 16

    across = {"node": flip(node, 1)}
    beside = {"node": flip(node, 2)}
    above = {"node": flip(node, 4)}
    partners = [across, beside, above]
    if four_rows:
        below = {"node": flip(node, 8)}
        partners.append(below)
    peers = [lax.rem(shard + k, shards) for k in range(1, shards)]
    partners += [{"shard": peer} for peer in peers]

    def token_rows(owner):
        return pl.ds(pl.multiple_of(owner * own_tokens, own_tokens), own_tokens)

    def acts_source(owner, part):
        start = pl.multiple_of(owner * own_rows + part * rows, 128)
        return hidden.at[0, :, pl.ds(start, rows)]

    def grads_source(part):
        return cotangent.at[0, :, pl.ds(pl.multiple_of(part * cols, 128), cols)]

    def own_acts(part):
        return pltpu.make_async_copy(
            acts_source(shard, part), acts.at[part, token_rows(shard)], acts_own.at[part])

    def own_grads(part):
        return pltpu.make_async_copy(
            grads_source(part), grads.at[part, token_rows(shard)], grads_own.at[part])

    def send_acts(part, k):
        slot = part * (shards - 1) + k
        return pltpu.make_async_remote_copy(
            acts_source(peers[k], part), acts.at[part, token_rows(shard)],
            acts_send.at[slot], acts_recv.at[slot],
            device_id={"shard": peers[k]}, device_id_type=pl.DeviceIdType.MESH)

    def send_grads(part, k):
        slot = part * (shards - 1) + k
        return pltpu.make_async_remote_copy(
            grads_source(part), grads.at[part, token_rows(shard)],
            grads_send.at[slot], grads_recv.at[slot],
            device_id={"shard": peers[k]}, device_id_type=pl.DeviceIdType.MESH)

    def place(array, tile):
        row = pl.multiple_of(lax.rem(tile, row_parts) * rows, 128)
        col = pl.multiple_of(lax.div(tile, row_parts) * cols, 128)
        return array.at[0, pl.ds(row, rows), pl.ds(col, cols)]

    def load_w(tile):
        return pltpu.make_async_copy(place(weights, tile), w_tiles.at[tile], w_sem.at[tile])

    def load_m(tile):
        return pltpu.make_async_copy(place(momentum, tile), m_tiles.at[tile], m_sem.at[tile])

    def store_w(tile):
        return pltpu.make_async_copy(w_tiles.at[tile], place(new_weights, tile), w_sem.at[tile])

    def store_m(tile):
        return pltpu.make_async_copy(m_tiles.at[tile], place(new_moment, tile), m_sem.at[tile])

    def exchange(source, target, send, recv, where, tile):
        return pltpu.make_async_remote_copy(
            source.at[tile], target.at[tile], send.at[tile], recv.at[tile],
            device_id=where, device_id_type=pl.DeviceIdType.MESH)

    to_west = functools.partial(exchange, h_tiles, west, west_send, west_recv, across)
    to_east = functools.partial(exchange, west, east, east_send, east_recv, beside)
    to_north = functools.partial(exchange, h_tiles, north, north_send, north_recv, above)
    if four_rows:
        to_south = functools.partial(exchange, north, south, south_send, south_recv, below)

    own_grads(0).start()

    @pl.loop(0, row_parts)
    def _(part):
        own_acts(part).start()

    @pl.loop(0, tiles)
    def _(tile):
        load_m(tile).start()
        load_w(tile).start()

    @pl.loop(1, col_parts)
    def _(part):
        own_grads(part).start()

    barrier = pltpu.get_barrier_semaphore()
    for partner in partners:
        pl.semaphore_signal(
            barrier, inc=1, device_id=partner, device_id_type=pl.DeviceIdType.MESH)
    pl.semaphore_wait(barrier, len(partners))

    for k in range(shards - 1):
        send_grads(0, k).start()

    @pl.loop(0, row_parts)
    def _(part):
        for k in range(shards - 1):
            send_acts(part, k).start()

    @pl.loop(1, col_parts)
    def _(part):
        for k in range(shards - 1):
            send_grads(part, k).start()

    strip = 32

    @pl.loop(0, tiles + FINAL_LAG)
    def _(step):
        @pl.when(step < tiles)
        def _():
            row_part = lax.rem(step, row_parts)
            col_part = lax.div(step, row_parts)

            @pl.when(row_part == 0)
            def _():
                own_grads(col_part).wait()
                for k in range(shards - 1):
                    send_grads(col_part, k).wait_recv()

            @pl.when(col_part == 0)
            def _():
                own_acts(row_part).wait()
                for k in range(shards - 1):
                    send_acts(row_part, k).wait_recv()

            load_m(step).wait()
            load_w(step).wait()
            product[...] = lax.dot_general(
                acts[row_part], grads[col_part], (((0,), (0,)), ((), ())),
                preferred_element_type=jnp.float32)

            @pl.loop(0, rows // strip)
            def _(index):
                at = pl.ds(pl.multiple_of(index * strip, strip), strip)
                moment = (
                    friction * m_tiles[step, at, :].astype(jnp.float32) + product[at, :]
                ).astype(jnp.bfloat16)
                m_tiles[step, at, :] = moment
                h_tiles[step, at, :] = (
                    w_tiles[step, at, :].astype(jnp.float32)
                    - step_size * moment.astype(jnp.float32)
                ).astype(jnp.bfloat16)

            to_north(step).start()
            to_west(step).start()
            store_m(step).start()

        @pl.when(jnp.logical_and(step >= RELAY_LAG, step < tiles + RELAY_LAG))
        def _():
            tile = step - RELAY_LAG
            to_west(tile).wait_recv()
            to_east(tile).start()
            if four_rows:
                to_north(tile).wait_recv()
                to_south(tile).start()

        @pl.when(step >= FINAL_LAG)
        def _():
            tile = step - FINAL_LAG
            to_east(tile).wait_recv()
            if four_rows:
                to_south(tile).wait_recv()
            else:
                to_north(tile).wait_recv()

            @pl.loop(0, rows // strip)
            def _(index):
                at = pl.ds(pl.multiple_of(index * strip, strip), strip)
                last = south if four_rows else north
                candidates = [
                    part[tile, at, :].astype(jnp.float32)
                    for part in (h_tiles, west, east, north, last)
                ]
                running = candidates[0]
                largest = candidates[0]
                smallest = candidates[0]
                for value in candidates[1:]:
                    running = running + value
                    largest = jnp.maximum(largest, value)
                    smallest = jnp.minimum(smallest, value)
                w_tiles[tile, at, :] = (
                    (running - largest - smallest) / 3.0
                ).astype(jnp.bfloat16)

            store_w(tile).start()

    @pl.loop(0, row_parts)
    def _(part):
        for k in range(shards - 1):
            send_acts(part, k).wait_send()

    @pl.loop(0, col_parts)
    def _(part):
        for k in range(shards - 1):
            send_grads(part, k).wait_send()

    @pl.loop(0, tiles)
    def _(tile):
        to_west(tile).wait_send()
        to_east(tile).wait_send()
        to_north(tile).wait_send()
        if four_rows:
            to_south(tile).wait_send()
        store_m(tile).wait()
        store_w(tile).wait()


def on_device(nodes, shards, hidden, cotangent, weights, momentum):
    _, own_tokens, _ = hidden.shape
    _, own_rows, features = weights.shape
    tokens = own_tokens * shards
    rows = largest_block(own_rows, 128, 256)
    cols = largest_block(features, 128, 512)
    row_parts, col_parts = own_rows // rows, features // cols
    tiles = row_parts * col_parts
    dma = pltpu.SemaphoreType.DMA
    tile_set = pltpu.VMEM((tiles, rows, cols), jnp.bfloat16)
    south_set = tile_set if nodes == 16 else pltpu.VMEM((1, 16, 128), jnp.bfloat16)
    south_sem = dma((tiles,)) if nodes == 16 else dma((1,))
    anywhere = pl.BlockSpec(memory_space=pl.ANY)
    return pl.pallas_call(
        functools.partial(kernel, nodes, shards, rows, cols),
        out_shape=(
            jax.ShapeDtypeStruct(weights.shape, jnp.bfloat16),
            jax.ShapeDtypeStruct(momentum.shape, jnp.bfloat16),
        ),
        in_specs=[anywhere] * 4,
        out_specs=(anywhere, anywhere),
        scratch_shapes=[
            pltpu.VMEM((row_parts, tokens, rows), jnp.bfloat16),
            pltpu.VMEM((col_parts, tokens, cols), jnp.bfloat16),
            tile_set, tile_set, tile_set, tile_set, tile_set, tile_set, south_set,
            pltpu.VMEM((rows, cols), jnp.float32),
            dma((row_parts,)),
            dma((row_parts * (shards - 1),)),
            dma((row_parts * (shards - 1),)),
            dma((col_parts,)),
            dma((col_parts * (shards - 1),)),
            dma((col_parts * (shards - 1),)),
            dma((tiles,)), dma((tiles,)),
            dma((tiles,)), dma((tiles,)),
            dma((tiles,)), dma((tiles,)),
            dma((tiles,)), dma((tiles,)),
            south_sem, south_sem,
        ],
        compiler_params=pltpu.CompilerParams(
            collective_id=0, has_side_effects=True, vmem_limit_bytes=58 * 2**20),
        cost_estimate=pl.CostEstimate(
            flops=2 * tokens * own_rows * features,
            bytes_accessed=8 * own_rows * features,
            transcendentals=0),
    )(hidden, cotangent, weights, momentum)


def solution(mesh):
    placed = P("node", "shard", None)
    return jax.shard_map(
        functools.partial(on_device, mesh.shape["node"], mesh.shape["shard"]),
        mesh=mesh,
        in_specs=(placed,) * 4,
        out_specs=(placed, placed),
        check_vma=False,
    )
```

```python
import functools

import jax
import jax.numpy as jnp
from jax import lax
from jax.experimental import pallas as pl
from jax.experimental.pallas import tpu as pltpu
from jax.sharding import PartitionSpec as P

step_size = 0.1
friction = 0.9
RELAY_LAG = 1
FINAL_LAG = 14


def flip(index, bit):
    return index + bit - 2 * bit * lax.rem(lax.div(index, bit), 2)


def largest_block(extent, unit, most):
    block = unit
    for size in range(unit, most + 1, unit):
        if extent % size == 0:
            block = size
    return block


def kernel(
    nodes, shards, rows, cols,
    hidden, cotangent, weights, momentum, w_all, m_all,
    acts, grads, h_tiles, west, east, north, south, product,
    acts_own, acts_send, acts_recv, grads_own, grads_send, grads_recv,
    w_sem, m_sem, west_send, west_recv, east_send, east_recv,
    north_send, north_recv, south_send, south_recv,
):
    node = lax.axis_index("node")
    shard = lax.axis_index("shard")
    row_parts, tokens, _ = acts.shape
    col_parts = grads.shape[0]
    own_tokens = tokens // shards
    tiles = row_parts * col_parts
    own_rows = rows * row_parts
    four_rows = nodes == 16
    strip = 32

    across = {"node": flip(node, 1)}
    beside = {"node": flip(node, 2)}
    above = {"node": flip(node, 4)}
    partners = [across, beside, above]
    if four_rows:
        below = {"node": flip(node, 8)}
        partners.append(below)
    peers = [lax.rem(shard + k, shards) for k in range(1, shards)]
    partners += [{"shard": peer} for peer in peers]

    def token_rows(owner):
        return pl.ds(pl.multiple_of(owner * own_tokens, own_tokens), own_tokens)

    def acts_source(owner, part):
        start = pl.multiple_of(owner * own_rows + part * rows, 128)
        return hidden.at[0, :, pl.ds(start, rows)]

    def grads_source(part):
        return cotangent.at[0, :, pl.ds(pl.multiple_of(part * cols, 128), cols)]

    def own_acts(part):
        return pltpu.make_async_copy(
            acts_source(shard, part), acts.at[part, token_rows(shard)], acts_own.at[part])

    def own_grads(part):
        return pltpu.make_async_copy(
            grads_source(part), grads.at[part, token_rows(shard)], grads_own.at[part])

    def send_acts(part, k):
        slot = part * (shards - 1) + k
        return pltpu.make_async_remote_copy(
            acts_source(peers[k], part), acts.at[part, token_rows(shard)],
            acts_send.at[slot], acts_recv.at[slot],
            device_id={"shard": peers[k]}, device_id_type=pl.DeviceIdType.MESH)

    def send_grads(part, k):
        slot = part * (shards - 1) + k
        return pltpu.make_async_remote_copy(
            grads_source(part), grads.at[part, token_rows(shard)],
            grads_send.at[slot], grads_recv.at[slot],
            device_id={"shard": peers[k]}, device_id_type=pl.DeviceIdType.MESH)

    def place(array, tile):
        row = pl.multiple_of(lax.rem(tile, row_parts) * rows, 128)
        col = pl.multiple_of(lax.div(tile, row_parts) * cols, 128)
        return array.at[0, pl.ds(row, rows), pl.ds(col, cols)]

    def strip_of(tile, index):
        row = pl.multiple_of(lax.rem(tile, row_parts) * rows + index * strip, strip)
        col = pl.multiple_of(lax.div(tile, row_parts) * cols, 128)
        return (0, pl.ds(row, strip), pl.ds(col, cols))

    def load_w(tile):
        return pltpu.make_async_copy(place(weights, tile), place(w_all, tile), w_sem.at[tile])

    def load_m(tile):
        return pltpu.make_async_copy(place(momentum, tile), place(m_all, tile), m_sem.at[tile])

    def exchange(source, target, send, recv, where, tile):
        return pltpu.make_async_remote_copy(
            source.at[tile], target.at[tile], send.at[tile], recv.at[tile],
            device_id=where, device_id_type=pl.DeviceIdType.MESH)

    to_west = functools.partial(exchange, h_tiles, west, west_send, west_recv, across)
    to_east = functools.partial(exchange, west, east, east_send, east_recv, beside)
    to_north = functools.partial(exchange, h_tiles, north, north_send, north_recv, above)
    if four_rows:
        to_south = functools.partial(exchange, north, south, south_send, south_recv, below)

    own_grads(0).start()

    @pl.loop(0, row_parts)
    def _(part):
        own_acts(part).start()

    @pl.loop(0, tiles)
    def _(tile):
        load_m(tile).start()
        load_w(tile).start()

    @pl.loop(1, col_parts)
    def _(part):
        own_grads(part).start()

    barrier = pltpu.get_barrier_semaphore()
    for partner in partners:
        pl.semaphore_signal(
            barrier, inc=1, device_id=partner, device_id_type=pl.DeviceIdType.MESH)
    pl.semaphore_wait(barrier, len(partners))

    for k in range(shards - 1):
        send_grads(0, k).start()

    @pl.loop(0, row_parts)
    def _(part):
        for k in range(shards - 1):
            send_acts(part, k).start()

    @pl.loop(1, col_parts)
    def _(part):
        for k in range(shards - 1):
            send_grads(part, k).start()

    @pl.loop(0, tiles + FINAL_LAG)
    def _(step):
        @pl.when(step < tiles)
        def _():
            row_part = lax.rem(step, row_parts)
            col_part = lax.div(step, row_parts)

            @pl.when(row_part == 0)
            def _():
                own_grads(col_part).wait()
                for k in range(shards - 1):
                    send_grads(col_part, k).wait_recv()

            @pl.when(col_part == 0)
            def _():
                own_acts(row_part).wait()
                for k in range(shards - 1):
                    send_acts(row_part, k).wait_recv()

            load_m(step).wait()
            load_w(step).wait()
            product[...] = lax.dot_general(
                acts[row_part], grads[col_part], (((0,), (0,)), ((), ())),
                preferred_element_type=jnp.float32)

            @pl.loop(0, rows // strip)
            def _(index):
                at = pl.ds(pl.multiple_of(index * strip, strip), strip)
                whole = strip_of(step, index)
                moment = (
                    friction * m_all[whole].astype(jnp.float32) + product[at, :]
                ).astype(jnp.bfloat16)
                m_all[whole] = moment
                h_tiles[step, at, :] = (
                    w_all[whole].astype(jnp.float32)
                    - step_size * moment.astype(jnp.float32)
                ).astype(jnp.bfloat16)

            to_north(step).start()
            to_west(step).start()

        @pl.when(jnp.logical_and(step >= RELAY_LAG, step < tiles + RELAY_LAG))
        def _():
            tile = step - RELAY_LAG
            to_west(tile).wait_recv()
            to_east(tile).start()
            if four_rows:
                to_north(tile).wait_recv()
                to_south(tile).start()

        @pl.when(step >= FINAL_LAG)
        def _():
            tile = step - FINAL_LAG
            to_east(tile).wait_recv()
            if four_rows:
                to_south(tile).wait_recv()
            else:
                to_north(tile).wait_recv()

            @pl.loop(0, rows // strip)
            def _(index):
                at = pl.ds(pl.multiple_of(index * strip, strip), strip)
                last = south if four_rows else north
                candidates = [
                    part[tile, at, :].astype(jnp.float32)
                    for part in (h_tiles, west, east, north, last)
                ]
                running = candidates[0]
                largest = candidates[0]
                smallest = candidates[0]
                for value in candidates[1:]:
                    running = running + value
                    largest = jnp.maximum(largest, value)
                    smallest = jnp.minimum(smallest, value)
                w_all[strip_of(tile, index)] = (
                    (running - largest - smallest) / 3.0
                ).astype(jnp.bfloat16)

    @pl.loop(0, row_parts)
    def _(part):
        for k in range(shards - 1):
            send_acts(part, k).wait_send()

    @pl.loop(0, col_parts)
    def _(part):
        for k in range(shards - 1):
            send_grads(part, k).wait_send()

    @pl.loop(0, tiles)
    def _(tile):
        to_west(tile).wait_send()
        to_east(tile).wait_send()
        to_north(tile).wait_send()
        if four_rows:
            to_south(tile).wait_send()


def on_device(nodes, shards, hidden, cotangent, weights, momentum):
    _, own_tokens, _ = hidden.shape
    _, own_rows, features = weights.shape
    tokens = own_tokens * shards
    rows = largest_block(own_rows, 128, 256)
    cols = largest_block(features, 128, 256)
    row_parts, col_parts = own_rows // rows, features // cols
    tiles = row_parts * col_parts
    dma = pltpu.SemaphoreType.DMA
    tile_set = pltpu.VMEM((tiles, rows, cols), jnp.bfloat16)
    south_set = tile_set if nodes == 16 else pltpu.VMEM((1, 16, 128), jnp.bfloat16)
    south_sem = dma((tiles,)) if nodes == 16 else dma((1,))
    in_hbm = pl.BlockSpec(memory_space=pltpu.HBM)
    in_vmem = pl.BlockSpec(memory_space=pltpu.VMEM)
    return pl.pallas_call(
        functools.partial(kernel, nodes, shards, rows, cols),
        out_shape=(
            pltpu.VMEM(weights.shape, jnp.bfloat16),
            pltpu.VMEM(momentum.shape, jnp.bfloat16),
        ),
        in_specs=[in_hbm] * 4,
        out_specs=(in_vmem, in_vmem),
        scratch_shapes=[
            pltpu.VMEM((row_parts, tokens, rows), jnp.bfloat16),
            pltpu.VMEM((col_parts, tokens, cols), jnp.bfloat16),
            tile_set, tile_set, tile_set, tile_set, south_set,
            pltpu.VMEM((rows, cols), jnp.float32),
            dma((row_parts,)),
            dma((row_parts * (shards - 1),)),
            dma((row_parts * (shards - 1),)),
            dma((col_parts,)),
            dma((col_parts * (shards - 1),)),
            dma((col_parts * (shards - 1),)),
            dma((tiles,)), dma((tiles,)),
            dma((tiles,)), dma((tiles,)),
            dma((tiles,)), dma((tiles,)),
            dma((tiles,)), dma((tiles,)),
            south_sem, south_sem,
        ],
        compiler_params=pltpu.CompilerParams(
            collective_id=0, has_side_effects=True, vmem_limit_bytes=40 * 2**20),
        cost_estimate=pl.CostEstimate(
            flops=2 * tokens * own_rows * features,
            bytes_accessed=8 * own_rows * features,
            transcendentals=0),
    )(hidden, cotangent, weights, momentum)


def solution(mesh):
    placed = P("node", "shard", None)
    return jax.shard_map(
        functools.partial(on_device, mesh.shape["node"], mesh.shape["shard"]),
        mesh=mesh,
        in_specs=(placed,) * 4,
        out_specs=(placed, placed),
        check_vma=False,
    )
```

```python
import functools

import jax
import jax.numpy as jnp
from jax import lax
from jax.experimental import pallas as pl
from jax.experimental.pallas import tpu as pltpu
from jax.sharding import PartitionSpec as P

step_size = 0.1
friction = 0.9
RELAY_LAG = 2
FINAL_LAG = 14
SEND_LAG = 4


def flip(index, bit):
    return index + bit - 2 * bit * lax.rem(lax.div(index, bit), 2)


def largest_block(extent, unit, most):
    block = unit
    for size in range(unit, most + 1, unit):
        if extent % size == 0:
            block = size
    return block


def kernel(
    nodes, shards, rows, cols,
    hidden, cotangent, weights, momentum, w_all, m_all,
    acts, grads, h_tiles, west, east, north, south, product,
    acts_own, acts_send, acts_recv, grads_own, grads_send, grads_recv,
    w_sem, m_sem, west_send, west_recv, east_send, east_recv,
    north_send, north_recv, south_send, south_recv,
):
    node = lax.axis_index("node")
    shard = lax.axis_index("shard")
    row_parts, tokens, _ = acts.shape
    col_parts = grads.shape[0]
    own_tokens = tokens // shards
    tiles = row_parts * col_parts
    own_rows = rows * row_parts
    four_rows = nodes == 16
    assert FINAL_LAG >= max(row_parts, col_parts) and tiles > FINAL_LAG
    strip = 32

    across = {"node": flip(node, 1)}
    beside = {"node": flip(node, 2)}
    above = {"node": flip(node, 4)}
    partners = [across, beside, above]
    if four_rows:
        below = {"node": flip(node, 8)}
        partners.append(below)
    peers = [lax.rem(shard + k, shards) for k in range(1, shards)]
    partners += [{"shard": peer} for peer in peers]

    def token_rows(owner):
        return pl.ds(pl.multiple_of(owner * own_tokens, own_tokens), own_tokens)

    def acts_source(owner, part):
        start = pl.multiple_of(owner * own_rows + part * rows, 128)
        return hidden.at[0, :, pl.ds(start, rows)]

    def grads_source(part):
        return cotangent.at[0, :, pl.ds(pl.multiple_of(part * cols, 128), cols)]

    def own_acts(part):
        return pltpu.make_async_copy(
            acts_source(shard, part), acts.at[part, token_rows(shard)], acts_own.at[part])

    def own_grads(part):
        return pltpu.make_async_copy(
            grads_source(part), grads.at[part, token_rows(shard)], grads_own.at[part])

    def send_acts(part, k):
        slot = part * (shards - 1) + k
        return pltpu.make_async_remote_copy(
            acts_source(peers[k], part), acts.at[part, token_rows(shard)],
            acts_send.at[slot], acts_recv.at[slot],
            device_id={"shard": peers[k]}, device_id_type=pl.DeviceIdType.MESH)

    def send_grads(part, k):
        slot = part * (shards - 1) + k
        return pltpu.make_async_remote_copy(
            grads_source(part), grads.at[part, token_rows(shard)],
            grads_send.at[slot], grads_recv.at[slot],
            device_id={"shard": peers[k]}, device_id_type=pl.DeviceIdType.MESH)

    def strip_of(tile, index):
        row = pl.multiple_of(lax.rem(tile, row_parts) * rows + index * strip, strip)
        col = pl.multiple_of(lax.div(tile, row_parts) * cols, 128)
        return (0, pl.ds(row, strip), pl.ds(col, cols))

    def column(array, part):
        return array.at[0, :, pl.ds(pl.multiple_of(part * cols, 128), cols)]

    def load_w(part):
        return pltpu.make_async_copy(column(weights, part), column(w_all, part), w_sem.at[part])

    def load_m(part):
        return pltpu.make_async_copy(column(momentum, part), column(m_all, part), m_sem.at[part])

    def exchange(source, target, send, recv, where, tile):
        return pltpu.make_async_remote_copy(
            source.at[tile], target.at[tile], send.at[tile], recv.at[tile],
            device_id=where, device_id_type=pl.DeviceIdType.MESH)

    to_west = functools.partial(exchange, h_tiles, west, west_send, west_recv, across)
    to_east = functools.partial(exchange, west, east, east_send, east_recv, beside)
    to_north = functools.partial(exchange, h_tiles, north, north_send, north_recv, above)
    if four_rows:
        to_south = functools.partial(exchange, north, south, south_send, south_recv, below)

    def wait_sends(tile):
        to_west(tile).wait_send()
        to_east(tile).wait_send()
        to_north(tile).wait_send()
        if four_rows:
            to_south(tile).wait_send()

    barrier = pltpu.get_barrier_semaphore()
    for partner in partners:
        pl.semaphore_signal(
            barrier, inc=1, device_id=partner, device_id_type=pl.DeviceIdType.MESH)
    own_grads(0).start()
    own_acts(0).start()
    load_m(0).start()
    load_w(0).start()
    pl.semaphore_wait(barrier, len(partners))

    for k in range(shards - 1):
        send_grads(0, k).start()

    @pl.loop(0, row_parts)
    def _(part):
        for k in range(shards - 1):
            send_acts(part, k).start()

    @pl.loop(1, row_parts)
    def _(part):
        own_acts(part).start()

    @pl.loop(1, col_parts)
    def _(part):
        for k in range(shards - 1):
            send_grads(part, k).start()
        own_grads(part).start()
        load_m(part).start()
        load_w(part).start()

    @pl.loop(0, tiles + FINAL_LAG)
    def _(step):
        @pl.when(step < tiles)
        def _():
            row_part = lax.rem(step, row_parts)
            col_part = lax.div(step, row_parts)

            @pl.when(row_part == 0)
            def _():
                own_grads(col_part).wait()
                for k in range(shards - 1):
                    send_grads(col_part, k).wait_recv()
                load_m(col_part).wait()
                load_w(col_part).wait()

            @pl.when(col_part == 0)
            def _():
                own_acts(row_part).wait()
                for k in range(shards - 1):
                    send_acts(row_part, k).wait_recv()

            product[...] = lax.dot_general(
                acts[row_part], grads[col_part], (((0,), (0,)), ((), ())),
                preferred_element_type=jnp.float32)

            @pl.loop(0, rows // strip)
            def _(index):
                at = pl.ds(pl.multiple_of(index * strip, strip), strip)
                whole = strip_of(step, index)
                moment = (
                    friction * m_all[whole].astype(jnp.float32) + product[at, :]
                ).astype(jnp.bfloat16)
                m_all[whole] = moment
                h_tiles[step, at, :] = (
                    w_all[whole].astype(jnp.float32)
                    - step_size * moment.astype(jnp.float32)
                ).astype(jnp.bfloat16)

            to_north(step).start()
            to_west(step).start()

        @pl.when(jnp.logical_and(step >= RELAY_LAG, step < tiles + RELAY_LAG))
        def _():
            tile = step - RELAY_LAG
            to_west(tile).wait_recv()
            to_east(tile).start()
            if four_rows:
                to_north(tile).wait_recv()
                to_south(tile).start()

        @pl.when(step >= FINAL_LAG)
        def _():
            tile = step - FINAL_LAG
            to_east(tile).wait_recv()
            if four_rows:
                to_south(tile).wait_recv()
            else:
                to_north(tile).wait_recv()

            @pl.loop(0, rows // strip)
            def _(index):
                at = pl.ds(pl.multiple_of(index * strip, strip), strip)
                last = south if four_rows else north
                candidates = [
                    part[tile, at, :].astype(jnp.float32)
                    for part in (h_tiles, west, east, north, last)
                ]
                running = candidates[0]
                largest = candidates[0]
                smallest = candidates[0]
                for value in candidates[1:]:
                    running = running + value
                    largest = jnp.maximum(largest, value)
                    smallest = jnp.minimum(smallest, value)
                w_all[strip_of(tile, index)] = (
                    (running - largest - smallest) / 3.0
                ).astype(jnp.bfloat16)

        @pl.when(jnp.logical_and(step >= tiles, step < tiles + row_parts))
        def _():
            for k in range(shards - 1):
                send_acts(step - tiles, k).wait_send()

        @pl.when(jnp.logical_and(step >= tiles, step < tiles + col_parts))
        def _():
            for k in range(shards - 1):
                send_grads(step - tiles, k).wait_send()

        @pl.when(step >= FINAL_LAG + SEND_LAG)
        def _():
            wait_sends(step - FINAL_LAG - SEND_LAG)

    @pl.loop(tiles - SEND_LAG, tiles)
    def _(tile):
        wait_sends(tile)

def on_device(nodes, shards, hidden, cotangent, weights, momentum):
    _, own_tokens, _ = hidden.shape
    _, own_rows, features = weights.shape
    tokens = own_tokens * shards
    rows = largest_block(own_rows, 128, 256)
    cols = largest_block(features, 128, 256)
    row_parts, col_parts = own_rows // rows, features // cols
    tiles = row_parts * col_parts
    dma = pltpu.SemaphoreType.DMA
    tile_set = pltpu.VMEM((tiles, rows, cols), jnp.bfloat16)
    south_set = tile_set if nodes == 16 else pltpu.VMEM((1, 16, 128), jnp.bfloat16)
    south_sem = dma((tiles,)) if nodes == 16 else dma((1,))
    in_hbm = pl.BlockSpec(memory_space=pltpu.HBM)
    in_vmem = pl.BlockSpec(memory_space=pltpu.VMEM)
    return pl.pallas_call(
        functools.partial(kernel, nodes, shards, rows, cols),
        out_shape=(
            pltpu.VMEM(weights.shape, jnp.bfloat16),
            pltpu.VMEM(momentum.shape, jnp.bfloat16),
        ),
        in_specs=[in_hbm] * 4,
        out_specs=(in_vmem, in_vmem),
        scratch_shapes=[
            pltpu.VMEM((row_parts, tokens, rows), jnp.bfloat16),
            pltpu.VMEM((col_parts, tokens, cols), jnp.bfloat16),
            tile_set, tile_set, tile_set, tile_set, south_set,
            pltpu.VMEM((rows, cols), jnp.float32),
            dma((row_parts,)),
            dma((row_parts * (shards - 1),)),
            dma((row_parts * (shards - 1),)),
            dma((col_parts,)),
            dma((col_parts * (shards - 1),)),
            dma((col_parts * (shards - 1),)),
            dma((col_parts,)), dma((col_parts,)),
            dma((tiles,)), dma((tiles,)),
            dma((tiles,)), dma((tiles,)),
            dma((tiles,)), dma((tiles,)),
            south_sem, south_sem,
        ],
        compiler_params=pltpu.CompilerParams(
            collective_id=0, has_side_effects=True, vmem_limit_bytes=40 * 2**20),
        cost_estimate=pl.CostEstimate(
            flops=2 * tokens * own_rows * features,
            bytes_accessed=8 * own_rows * features,
            transcendentals=0),
    )(hidden, cotangent, weights, momentum)


def solution(mesh):
    placed = P("node", "shard", None)
    return jax.shard_map(
        functools.partial(on_device, mesh.shape["node"], mesh.shape["shard"]),
        mesh=mesh,
        in_specs=(placed,) * 4,
        out_specs=(placed, placed),
        check_vma=False,
    )
```

```python
import functools

import jax
import jax.numpy as jnp
from jax import lax
from jax.experimental import pallas as pl
from jax.experimental.pallas import tpu as pltpu
from jax.sharding import PartitionSpec as P

step_size = 0.1
friction = 0.9
RELAY_LAG = 2
FINAL_LAG = 14
SEND_LAG = 4


def flip(index, bit):
    return index + bit - 2 * bit * lax.rem(lax.div(index, bit), 2)


def largest_block(extent, unit, most):
    block = unit
    for size in range(unit, most + 1, unit):
        if extent % size == 0:
            block = size
    return block


def kernel(
    nodes, shards, rows, cols,
    hidden, cotangent, weights, momentum, w_all, m_all,
    acts, grads, h_tiles, west, east, north, spare, product,
    acts_own, acts_send, acts_recv, grads_own, grads_send, grads_recv,
    w_sem, m_sem, west_send, west_recv, east_send, east_recv,
    north_send, north_recv, spare_send, spare_recv, over_send, side_send,
):
    node = lax.axis_index("node")
    shard = lax.axis_index("shard")
    row_parts, tokens, _ = acts.shape
    col_parts = grads.shape[0]
    own_tokens = tokens // shards
    tiles = row_parts * col_parts
    own_rows = rows * row_parts
    four_rows = nodes == 16
    assert FINAL_LAG >= max(row_parts, col_parts) and tiles > FINAL_LAG
    strip = 32

    across = {"node": flip(node, 1)}
    beside = {"node": flip(node, 2)}
    above = {"node": flip(node, 4)}
    if four_rows:
        below = {"node": flip(node, 8)}
    else:
        below = {"node": flip(flip(node, 4), 2)}
    partners = [across, beside, above, below]
    inner = lax.rem(lax.div(node, 2) + lax.div(node, 4), 2) == 1
    outer = jnp.logical_not(inner)

    def even(tile):
        return lax.rem(tile, 2) == 0
    peers = [lax.rem(shard + k, shards) for k in range(1, shards)]
    partners += [{"shard": peer} for peer in peers]

    def token_rows(owner):
        return pl.ds(pl.multiple_of(owner * own_tokens, own_tokens), own_tokens)

    def acts_source(owner, part):
        start = pl.multiple_of(owner * own_rows + part * rows, 128)
        return hidden.at[0, :, pl.ds(start, rows)]

    def grads_source(part):
        return cotangent.at[0, :, pl.ds(pl.multiple_of(part * cols, 128), cols)]

    def own_acts(part):
        return pltpu.make_async_copy(
            acts_source(shard, part), acts.at[part, token_rows(shard)], acts_own.at[part])

    def own_grads(part):
        return pltpu.make_async_copy(
            grads_source(part), grads.at[part, token_rows(shard)], grads_own.at[part])

    def send_acts(part, k):
        slot = part * (shards - 1) + k
        return pltpu.make_async_remote_copy(
            acts_source(peers[k], part), acts.at[part, token_rows(shard)],
            acts_send.at[slot], acts_recv.at[slot],
            device_id={"shard": peers[k]}, device_id_type=pl.DeviceIdType.MESH)

    def send_grads(part, k):
        slot = part * (shards - 1) + k
        return pltpu.make_async_remote_copy(
            grads_source(part), grads.at[part, token_rows(shard)],
            grads_send.at[slot], grads_recv.at[slot],
            device_id={"shard": peers[k]}, device_id_type=pl.DeviceIdType.MESH)

    def strip_of(tile, index):
        row = pl.multiple_of(lax.rem(tile, row_parts) * rows + index * strip, strip)
        col = pl.multiple_of(lax.div(tile, row_parts) * cols, 128)
        return (0, pl.ds(row, strip), pl.ds(col, cols))

    def column(array, part):
        return array.at[0, :, pl.ds(pl.multiple_of(part * cols, 128), cols)]

    def load_w(part):
        return pltpu.make_async_copy(column(weights, part), column(w_all, part), w_sem.at[part])

    def load_m(part):
        return pltpu.make_async_copy(column(momentum, part), column(m_all, part), m_sem.at[part])

    def exchange(source, target, send, recv, where, tile):
        return pltpu.make_async_remote_copy(
            source.at[tile], target.at[tile], send.at[tile], recv.at[tile],
            device_id=where, device_id_type=pl.DeviceIdType.MESH)

    to_west = functools.partial(exchange, h_tiles, west, west_send, west_recv, across)
    to_east = functools.partial(exchange, west, east, east_send, east_recv, beside)
    to_north = functools.partial(exchange, h_tiles, north, north_send, north_recv, above)
    if four_rows:
        to_south = functools.partial(exchange, north, spare, spare_send, spare_recv, below)
    else:
        to_inner = functools.partial(exchange, h_tiles, spare, spare_send, spare_recv, beside)
        over_cut = functools.partial(exchange, spare, north, over_send, north_recv, below)
        sideways = functools.partial(exchange, spare, east, side_send, east_recv, across)

    def wait_sends(tile):
        to_west(tile).wait_send()
        if four_rows:
            to_east(tile).wait_send()
            to_north(tile).wait_send()
            to_south(tile).wait_send()
            return

        @pl.when(inner)
        def _():
            to_east(tile).wait_send()
            to_north(tile).wait_send()
            over_cut(tile).wait_send()

            @pl.when(even(tile))
            def _():
                sideways(tile).wait_send()

        @pl.when(outer)
        def _():
            to_inner(tile).wait_send()

            @pl.when(jnp.logical_not(even(tile)))
            def _():
                to_east(tile).wait_send()

    barrier = pltpu.get_barrier_semaphore()
    for partner in partners:
        pl.semaphore_signal(
            barrier, inc=1, device_id=partner, device_id_type=pl.DeviceIdType.MESH)
    own_grads(0).start()
    own_acts(0).start()
    load_m(0).start()
    load_w(0).start()
    pl.semaphore_wait(barrier, len(partners))

    for k in range(shards - 1):
        send_grads(0, k).start()

    @pl.loop(0, row_parts)
    def _(part):
        for k in range(shards - 1):
            send_acts(part, k).start()

    @pl.loop(1, row_parts)
    def _(part):
        own_acts(part).start()

    @pl.loop(1, col_parts)
    def _(part):
        for k in range(shards - 1):
            send_grads(part, k).start()
        own_grads(part).start()
        load_m(part).start()
        load_w(part).start()

    @pl.loop(0, tiles + FINAL_LAG)
    def _(step):
        @pl.when(step < tiles)
        def _():
            row_part = lax.rem(step, row_parts)
            col_part = lax.div(step, row_parts)

            @pl.when(row_part == 0)
            def _():
                own_grads(col_part).wait()
                for k in range(shards - 1):
                    send_grads(col_part, k).wait_recv()
                load_m(col_part).wait()
                load_w(col_part).wait()

            @pl.when(col_part == 0)
            def _():
                own_acts(row_part).wait()
                for k in range(shards - 1):
                    send_acts(row_part, k).wait_recv()

            product[...] = lax.dot_general(
                acts[row_part], grads[col_part], (((0,), (0,)), ((), ())),
                preferred_element_type=jnp.float32)

            @pl.loop(0, rows // strip)
            def _(index):
                at = pl.ds(pl.multiple_of(index * strip, strip), strip)
                whole = strip_of(step, index)
                moment = (
                    friction * m_all[whole].astype(jnp.float32) + product[at, :]
                ).astype(jnp.bfloat16)
                m_all[whole] = moment
                h_tiles[step, at, :] = (
                    w_all[whole].astype(jnp.float32)
                    - step_size * moment.astype(jnp.float32)
                ).astype(jnp.bfloat16)

            if four_rows:
                to_north(step).start()
            else:
                @pl.when(inner)
                def _():
                    to_north(step).start()

                @pl.when(outer)
                def _():
                    to_inner(step).start()

            to_west(step).start()

        @pl.when(jnp.logical_and(step >= RELAY_LAG, step < tiles + RELAY_LAG))
        def _():
            tile = step - RELAY_LAG
            if four_rows:
                to_west(tile).wait_recv()
                to_east(tile).start()
                to_north(tile).wait_recv()
                to_south(tile).start()
            else:
                @pl.when(inner)
                def _():
                    to_inner(tile).wait_recv()
                    over_cut(tile).start()

                    @pl.when(even(tile))
                    def _():
                        sideways(tile).start()

                to_west(tile).wait_recv()

                @pl.when(jnp.logical_or(inner, jnp.logical_not(even(tile))))
                def _():
                    to_east(tile).start()

        @pl.when(step >= FINAL_LAG)
        def _():
            tile = step - FINAL_LAG
            to_east(tile).wait_recv()
            if four_rows:
                to_south(tile).wait_recv()
            else:
                to_north(tile).wait_recv()

            @pl.loop(0, rows // strip)
            def _(index):
                at = pl.ds(pl.multiple_of(index * strip, strip), strip)
                last = spare if four_rows else north
                candidates = [
                    part[tile, at, :].astype(jnp.float32)
                    for part in (h_tiles, west, east, north, last)
                ]
                running = candidates[0]
                largest = candidates[0]
                smallest = candidates[0]
                for value in candidates[1:]:
                    running = running + value
                    largest = jnp.maximum(largest, value)
                    smallest = jnp.minimum(smallest, value)
                w_all[strip_of(tile, index)] = (
                    (running - largest - smallest) / 3.0
                ).astype(jnp.bfloat16)

        @pl.when(jnp.logical_and(step >= tiles, step < tiles + row_parts))
        def _():
            for k in range(shards - 1):
                send_acts(step - tiles, k).wait_send()

        @pl.when(jnp.logical_and(step >= tiles, step < tiles + col_parts))
        def _():
            for k in range(shards - 1):
                send_grads(step - tiles, k).wait_send()

        @pl.when(step >= FINAL_LAG + SEND_LAG)
        def _():
            wait_sends(step - FINAL_LAG - SEND_LAG)

    @pl.loop(tiles - SEND_LAG, tiles)
    def _(tile):
        wait_sends(tile)

def on_device(nodes, shards, hidden, cotangent, weights, momentum):
    _, own_tokens, _ = hidden.shape
    _, own_rows, features = weights.shape
    tokens = own_tokens * shards
    rows = largest_block(own_rows, 128, 256)
    cols = largest_block(features, 128, 256)
    row_parts, col_parts = own_rows // rows, features // cols
    tiles = row_parts * col_parts
    dma = pltpu.SemaphoreType.DMA
    tile_set = pltpu.VMEM((tiles, rows, cols), jnp.bfloat16)
    in_hbm = pl.BlockSpec(memory_space=pltpu.HBM)
    in_vmem = pl.BlockSpec(memory_space=pltpu.VMEM)
    return pl.pallas_call(
        functools.partial(kernel, nodes, shards, rows, cols),
        out_shape=(
            pltpu.VMEM(weights.shape, jnp.bfloat16),
            pltpu.VMEM(momentum.shape, jnp.bfloat16),
        ),
        in_specs=[in_hbm] * 4,
        out_specs=(in_vmem, in_vmem),
        scratch_shapes=[
            pltpu.VMEM((row_parts, tokens, rows), jnp.bfloat16),
            pltpu.VMEM((col_parts, tokens, cols), jnp.bfloat16),
            tile_set, tile_set, tile_set, tile_set, tile_set,
            pltpu.VMEM((rows, cols), jnp.float32),
            dma((row_parts,)),
            dma((row_parts * (shards - 1),)),
            dma((row_parts * (shards - 1),)),
            dma((col_parts,)),
            dma((col_parts * (shards - 1),)),
            dma((col_parts * (shards - 1),)),
            dma((col_parts,)), dma((col_parts,)),
            dma((tiles,)), dma((tiles,)),
            dma((tiles,)), dma((tiles,)),
            dma((tiles,)), dma((tiles,)),
            dma((tiles,)), dma((tiles,)), dma((tiles,)), dma((tiles,)),
        ],
        compiler_params=pltpu.CompilerParams(
            collective_id=0, has_side_effects=True, vmem_limit_bytes=45 * 2**20),
        cost_estimate=pl.CostEstimate(
            flops=2 * tokens * own_rows * features,
            bytes_accessed=8 * own_rows * features,
            transcendentals=0),
    )(hidden, cotangent, weights, momentum)


def solution(mesh):
    placed = P("node", "shard", None)
    return jax.shard_map(
        functools.partial(on_device, mesh.shape["node"], mesh.shape["shard"]),
        mesh=mesh,
        in_specs=(placed,) * 4,
        out_specs=(placed, placed),
        check_vma=False,
    )
```

```python
import functools

import jax
import jax.numpy as jnp
from jax import lax
from jax.experimental import pallas as pl
from jax.experimental.pallas import tpu as pltpu
from jax.sharding import PartitionSpec as P

step_size = 0.1
friction = 0.9
RELAY_LAG = 2
FINAL_LAG = 14
SEND_LAG = 4


def flip(index, bit):
    return index + bit - 2 * bit * lax.rem(lax.div(index, bit), 2)


def largest_block(extent, unit, most):
    block = unit
    for size in range(unit, most + 1, unit):
        if extent % size == 0:
            block = size
    return block


def kernel(
    nodes, shards, rows, cols,
    hidden, cotangent, weights, momentum, w_all, m_all,
    acts, grads, h_tiles, west, east, north, spare, product,
    acts_own, acts_send, acts_recv, grads_own, grads_send, grads_recv,
    w_sem, m_sem, west_send, west_recv, east_send, east_recv,
    north_send, north_recv, spare_send, spare_recv, over_send, side_send,
):
    node = lax.axis_index("node")
    shard = lax.axis_index("shard")
    row_parts, tokens, _ = acts.shape
    col_parts = grads.shape[0]
    own_tokens = tokens // shards
    tiles = row_parts * col_parts
    own_rows = rows * row_parts
    four_rows = nodes == 16
    assert FINAL_LAG >= max(row_parts, col_parts) and tiles > FINAL_LAG
    strip = 32

    across = {"node": flip(node, 1)}
    beside = {"node": flip(node, 2)}
    above = {"node": flip(node, 4)}
    if four_rows:
        below = {"node": flip(node, 8)}
    else:
        below = {"node": flip(flip(node, 4), 2)}
    partners = [across, beside, above, below]
    inner = lax.rem(lax.div(node, 2) + lax.div(node, 4), 2) == 1
    outer = jnp.logical_not(inner)

    def even(tile):
        return lax.rem(tile, 2) == 0
    peers = [lax.rem(shard + k, shards) for k in range(1, shards)]
    partners += [{"shard": peer} for peer in peers]

    def token_rows(owner):
        return pl.ds(pl.multiple_of(owner * own_tokens, own_tokens), own_tokens)

    def acts_source(owner, part):
        start = pl.multiple_of(owner * own_rows + part * rows, 128)
        return hidden.at[0, :, pl.ds(start, rows)]

    def grads_source(part):
        return cotangent.at[0, :, pl.ds(pl.multiple_of(part * cols, 128), cols)]

    def own_acts(part):
        return pltpu.make_async_copy(
            acts_source(shard, part), acts.at[part, token_rows(shard)], acts_own.at[part])

    def own_grads(part):
        return pltpu.make_async_copy(
            grads_source(part), grads.at[part, token_rows(shard)], grads_own.at[part])

    def send_acts(part, k):
        slot = part * (shards - 1) + k
        return pltpu.make_async_remote_copy(
            acts_source(peers[k], part), acts.at[part, token_rows(shard)],
            acts_send.at[slot], acts_recv.at[slot],
            device_id={"shard": peers[k]}, device_id_type=pl.DeviceIdType.MESH)

    def send_grads(part, k):
        slot = part * (shards - 1) + k
        return pltpu.make_async_remote_copy(
            grads_source(part), grads.at[part, token_rows(shard)],
            grads_send.at[slot], grads_recv.at[slot],
            device_id={"shard": peers[k]}, device_id_type=pl.DeviceIdType.MESH)

    def strip_of(tile, index):
        row = pl.multiple_of(lax.rem(tile, row_parts) * rows + index * strip, strip)
        col = pl.multiple_of(lax.div(tile, row_parts) * cols, 128)
        return (0, pl.ds(row, strip), pl.ds(col, cols))

    def column(array, part):
        return array.at[0, :, pl.ds(pl.multiple_of(part * cols, 128), cols)]

    def load_w(part):
        return pltpu.make_async_copy(column(weights, part), column(w_all, part), w_sem.at[part])

    def load_m(part):
        return pltpu.make_async_copy(column(momentum, part), column(m_all, part), m_sem.at[part])

    def exchange(source, target, send, recv, where, tile):
        return pltpu.make_async_remote_copy(
            source.at[tile], target.at[tile], send.at[tile], recv.at[tile],
            device_id=where, device_id_type=pl.DeviceIdType.MESH)

    to_west = functools.partial(exchange, h_tiles, west, west_send, west_recv, across)
    to_east = functools.partial(exchange, west, east, east_send, east_recv, beside)
    to_north = functools.partial(exchange, h_tiles, north, north_send, north_recv, above)
    if four_rows:
        to_south = functools.partial(exchange, north, spare, spare_send, spare_recv, below)
    else:
        to_inner = functools.partial(exchange, h_tiles, spare, spare_send, spare_recv, beside)
        over_cut = functools.partial(exchange, spare, north, over_send, north_recv, below)
        sideways = functools.partial(exchange, spare, east, side_send, east_recv, across)

    def wait_sends(tile):
        to_west(tile).wait_send()
        if four_rows:
            to_east(tile).wait_send()
            to_north(tile).wait_send()
            to_south(tile).wait_send()
            return

        @pl.when(inner)
        def _():
            to_east(tile).wait_send()
            to_north(tile).wait_send()
            over_cut(tile).wait_send()

            @pl.when(even(tile))
            def _():
                sideways(tile).wait_send()

        @pl.when(outer)
        def _():
            to_inner(tile).wait_send()

            @pl.when(jnp.logical_not(even(tile)))
            def _():
                to_east(tile).wait_send()

    barrier = pltpu.get_barrier_semaphore()
    for partner in partners:
        pl.semaphore_signal(
            barrier, inc=1, device_id=partner, device_id_type=pl.DeviceIdType.MESH)
    own_grads(0).start()
    own_acts(0).start()
    load_m(0).start()
    load_w(0).start()
    pl.semaphore_wait(barrier, len(partners))

    for k in range(shards - 1):
        send_grads(0, k).start()

    @pl.loop(0, row_parts)
    def _(part):
        for k in range(shards - 1):
            send_acts(part, k).start()

    @pl.loop(1, row_parts)
    def _(part):
        own_acts(part).start()

    @pl.loop(0, tiles + FINAL_LAG)
    def _(step):
        @pl.when(step < tiles)
        def _():
            row_part = lax.rem(step, row_parts)
            col_part = lax.div(step, row_parts)

            @pl.when(row_part == 0)
            def _():
                own_grads(col_part).wait()
                for k in range(shards - 1):
                    send_grads(col_part, k).wait_recv()
                load_m(col_part).wait()
                load_w(col_part).wait()

            @pl.when(col_part == 0)
            def _():
                own_acts(row_part).wait()
                for k in range(shards - 1):
                    send_acts(row_part, k).wait_recv()

            product[...] = lax.dot_general(
                acts[row_part], grads[col_part], (((0,), (0,)), ((), ())),
                preferred_element_type=jnp.float32)

            @pl.loop(0, rows // strip)
            def _(index):
                at = pl.ds(pl.multiple_of(index * strip, strip), strip)
                whole = strip_of(step, index)
                moment = (
                    friction * m_all[whole].astype(jnp.float32) + product[at, :]
                ).astype(jnp.bfloat16)
                m_all[whole] = moment
                h_tiles[step, at, :] = (
                    w_all[whole].astype(jnp.float32)
                    - step_size * moment.astype(jnp.float32)
                ).astype(jnp.bfloat16)

            if four_rows:
                to_north(step).start()
            else:
                @pl.when(inner)
                def _():
                    to_north(step).start()

                @pl.when(outer)
                def _():
                    to_inner(step).start()

            to_west(step).start()

            @pl.when(step < col_parts - 1)
            def _():
                for k in range(shards - 1):
                    send_grads(step + 1, k).start()
                own_grads(step + 1).start()
                load_m(step + 1).start()
                load_w(step + 1).start()

        @pl.when(jnp.logical_and(step >= RELAY_LAG, step < tiles + RELAY_LAG))
        def _():
            tile = step - RELAY_LAG
            if four_rows:
                to_west(tile).wait_recv()
                to_east(tile).start()
                to_north(tile).wait_recv()
                to_south(tile).start()
            else:
                @pl.when(inner)
                def _():
                    to_inner(tile).wait_recv()
                    over_cut(tile).start()

                    @pl.when(even(tile))
                    def _():
                        sideways(tile).start()

                to_west(tile).wait_recv()

                @pl.when(jnp.logical_or(inner, jnp.logical_not(even(tile))))
                def _():
                    to_east(tile).start()

        @pl.when(step >= FINAL_LAG)
        def _():
            tile = step - FINAL_LAG
            to_east(tile).wait_recv()
            if four_rows:
                to_south(tile).wait_recv()
            else:
                to_north(tile).wait_recv()

            @pl.loop(0, rows // strip)
            def _(index):
                at = pl.ds(pl.multiple_of(index * strip, strip), strip)
                last = spare if four_rows else north
                candidates = [
                    part[tile, at, :].astype(jnp.float32)
                    for part in (h_tiles, west, east, north, last)
                ]
                running = candidates[0]
                largest = candidates[0]
                smallest = candidates[0]
                for value in candidates[1:]:
                    running = running + value
                    largest = jnp.maximum(largest, value)
                    smallest = jnp.minimum(smallest, value)
                w_all[strip_of(tile, index)] = (
                    (running - largest - smallest) / 3.0
                ).astype(jnp.bfloat16)

        @pl.when(jnp.logical_and(step >= tiles, step < tiles + row_parts))
        def _():
            for k in range(shards - 1):
                send_acts(step - tiles, k).wait_send()

        @pl.when(jnp.logical_and(step >= tiles, step < tiles + col_parts))
        def _():
            for k in range(shards - 1):
                send_grads(step - tiles, k).wait_send()

        @pl.when(step >= FINAL_LAG + SEND_LAG)
        def _():
            wait_sends(step - FINAL_LAG - SEND_LAG)

    @pl.loop(tiles - SEND_LAG, tiles)
    def _(tile):
        wait_sends(tile)

def write_out(rows, w_all, m_all, new_weights, new_moment, sem):
    copies = []
    for part in range(w_all.shape[1] // rows):
        at = pl.ds(part * rows, rows)
        copies.append(pltpu.make_async_copy(
            w_all.at[:, at, :], new_weights.at[:, at, :], sem.at[2 * part]))
        copies.append(pltpu.make_async_copy(
            m_all.at[:, at, :], new_moment.at[:, at, :], sem.at[2 * part + 1]))
    for copy in copies:
        copy.start()
    for copy in copies:
        copy.wait()


def on_device(nodes, shards, hidden, cotangent, weights, momentum):
    _, own_tokens, _ = hidden.shape
    _, own_rows, features = weights.shape
    tokens = own_tokens * shards
    rows = largest_block(own_rows, 128, 256)
    cols = largest_block(features, 128, 256)
    row_parts, col_parts = own_rows // rows, features // cols
    tiles = row_parts * col_parts
    dma = pltpu.SemaphoreType.DMA
    tile_set = pltpu.VMEM((tiles, rows, cols), jnp.bfloat16)
    in_hbm = pl.BlockSpec(memory_space=pltpu.HBM)
    in_vmem = pl.BlockSpec(memory_space=pltpu.VMEM)
    results = pl.pallas_call(
        functools.partial(kernel, nodes, shards, rows, cols),
        out_shape=(
            pltpu.VMEM(weights.shape, jnp.bfloat16),
            pltpu.VMEM(momentum.shape, jnp.bfloat16),
        ),
        in_specs=[in_hbm] * 4,
        out_specs=(in_vmem, in_vmem),
        scratch_shapes=[
            pltpu.VMEM((row_parts, tokens, rows), jnp.bfloat16),
            pltpu.VMEM((col_parts, tokens, cols), jnp.bfloat16),
            tile_set, tile_set, tile_set, tile_set, tile_set,
            pltpu.VMEM((rows, cols), jnp.float32),
            dma((row_parts,)),
            dma((row_parts * (shards - 1),)),
            dma((row_parts * (shards - 1),)),
            dma((col_parts,)),
            dma((col_parts * (shards - 1),)),
            dma((col_parts * (shards - 1),)),
            dma((col_parts,)), dma((col_parts,)),
            dma((tiles,)), dma((tiles,)),
            dma((tiles,)), dma((tiles,)),
            dma((tiles,)), dma((tiles,)),
            dma((tiles,)), dma((tiles,)), dma((tiles,)), dma((tiles,)),
        ],
        compiler_params=pltpu.CompilerParams(
            collective_id=0, has_side_effects=True, vmem_limit_bytes=45 * 2**20),
        cost_estimate=pl.CostEstimate(
            flops=2 * tokens * own_rows * features,
            bytes_accessed=8 * own_rows * features,
            transcendentals=0),
    )(hidden, cotangent, weights, momentum)
    anywhere = pl.BlockSpec(memory_space=pl.ANY)
    return pl.pallas_call(
        functools.partial(write_out, rows),
        out_shape=(
            jax.ShapeDtypeStruct(weights.shape, jnp.bfloat16),
            jax.ShapeDtypeStruct(momentum.shape, jnp.bfloat16),
        ),
        in_specs=[anywhere] * 2,
        out_specs=(in_hbm, in_hbm),
        scratch_shapes=[dma((2 * row_parts,))],
        compiler_params=pltpu.CompilerParams(vmem_limit_bytes=2**20),
    )(*results)


def solution(mesh):
    placed = P("node", "shard", None)
    return jax.shard_map(
        functools.partial(on_device, mesh.shape["node"], mesh.shape["shard"]),
        mesh=mesh,
        in_specs=(placed,) * 4,
        out_specs=(placed, placed),
        check_vma=False,
    )
```
